32 devices in a mesh: row: 4 (over z), col: 8 (over y, x, core).
Axes of the slice: x: 2, y: 2, z: 4, core: 2. Of those that a mesh axis runs over, the one named last changes fastest.
Arguments:
- child_rhs: bfloat16 [2, 16384, 256], P(None, 'row', 'col'), may hold values from -6 to 6
- child_inverse_t: bfloat16 [2, 16384, 8192], P(None, 'row', 'col'), may hold values from -0.046875 to 0.046875
- boundary_tiles: bfloat16 [2, 16384, 8192], P(None, 'row', 'col'), may hold values from -0.046875 to 0.046875
- boundary_lists: int32 [2, 64], replicated, may hold values from 0 to 95, as said below
- root_rhs: bfloat16 [2, 12288, 256], P(None, 'col'), may hold values from -6 to 6
- root_inverse: bfloat16 [2, 12288, 12288], P(None, 'row', 'col'), may hold values from -0.0390625 to 0.0390625
Outputs:
- child_solution: bfloat16 [2, 8192, 512], P(None, 'col', 'row')
- root_solution: float32 [2, 12288, 256], P(None, 'row', 'col')
The draws below stay inside these ranges and needn't reach their ends.
Inputs may be any that keep to these rules, and one draw needn't show every extreme that they name: `boundary_lists`: within one child the 64 entries name distinct root blocks; the two children together name every one of the 96 root blocks.
All inputs are finite; a program needn't handle non-finite values.
Results may differ from the reference program's by a relative error of at most 0.0055.
Values may be sent and summed in bfloat16 or wider, within the bound.
No kernel may reach another device: no remote copies, remote signals or barrier semaphores. Data moves between devices by JAX's collectives and lax.ppermute only.
A program may use at most 128 MiB of HBM per device.

```python
import jax
import jax.numpy as jnp
from jax import lax

P_SIZE = 8192
CB = 8192
R = 12288
NRHS = 256
BLK = 128
NBLK = 64
RB = 96


def draw_boundary_lists(key, part):
    order = jax.random.permutation(key, RB).astype(jnp.int32)
    first_child = order[:NBLK]
    second_child = jax.random.permutation(jax.random.fold_in(key, 7), order[RB - NBLK:]).astype(jnp.int32)
    return jnp.stack((first_child, second_child)).astype(jnp.int32)


def level_of(rng, dims, split, smallest, largest):
    def one(axis_at, blocks):
        steps = jax.random.uniform(jax.random.fold_in(jax.random.fold_in(rng, 6), axis_at), (blocks,), jnp.float32, smallest / len(split), largest / len(split))
        return jnp.repeat(jnp.exp(steps), dims[axis_at] // blocks).reshape((-1,) + (1,) * (len(dims) - axis_at - 1))

    gain = one(*split[0])
    for cut in split[1:]:
        gain = gain * one(*cut)
    return gain


def gaussian(own_key, dims, width, limit, split=(), held_as=jnp.bfloat16):
    entries = jax.random.normal(own_key, dims, jnp.float32) * width
    if len(split) > 0:
        entries = level_of(own_key, dims, split, -0.22, 0.18) * entries
    return jnp.clip(entries, min=-limit, max=limit).astype(held_as)


def setup_inputs(seed: int = 0) -> dict:
    streams_of = jax.random.split(jax.random.key(seed), 7)
    return {
        "child_rhs": gaussian(streams_of[0], (2, 2 * P_SIZE, NRHS), 1.0, 6.0, ((1, 4), (2, 8))),
        "child_inverse_t": gaussian(streams_of[1], (2, 2 * P_SIZE, P_SIZE), (2 * P_SIZE) ** -0.5, 0.046875, ((1, 4), (2, 8))),
        "boundary_tiles": gaussian(streams_of[2], (2, 2 * CB, P_SIZE), (2 * P_SIZE) ** -0.5, 0.046875, ((1, 4), (2, 8))),
        "boundary_lists": draw_boundary_lists(jax.random.fold_in(streams_of[6], 71), 0),
        "root_rhs": gaussian(streams_of[4], (2, R, NRHS), 1.0, 6.0, ((1, 8),)),
        "root_inverse": gaussian(streams_of[5], (2, R, R), (2 * R) ** -0.5, 0.0390625, ((1, 4), (2, 8))),
    }


def turned_dot(left, right):
    return lax.dot_general(left, right, (((0,), (0,)), ((), ())), preferred_element_type=jnp.float32)


def plain_dot(left, right):
    return jnp.dot(left, right, preferred_element_type=jnp.float32)


def reference(child_rhs, child_inverse_t, boundary_tiles, boundary_lists, root_rhs, root_inverse):
    solutions = []
    assembled = jnp.zeros((2, RB, BLK, NRHS), jnp.float32)
    for child in range(2):
        inverse_part = child_inverse_t[:, child * P_SIZE:(child + 1) * P_SIZE, :]
        rhs_part = child_rhs[:, child * P_SIZE:(child + 1) * P_SIZE, :]
        real_part = turned_dot(inverse_part[0], rhs_part[0]) - turned_dot(inverse_part[1], rhs_part[1])
        imag_part = turned_dot(inverse_part[0], rhs_part[1]) + turned_dot(inverse_part[1], rhs_part[0])
        solution = jnp.stack((real_part, imag_part)).astype(jnp.bfloat16)
        solutions.append(solution)
        tiles = boundary_tiles[:, child * CB:(child + 1) * CB, :]
        update_real = plain_dot(tiles[0], solution[0]) - plain_dot(tiles[1], solution[1])
        update_imag = plain_dot(tiles[0], solution[1]) + plain_dot(tiles[1], solution[0])
        update = jnp.stack((update_real, update_imag)).astype(jnp.bfloat16)
        blocks = update.astype(jnp.float32).reshape(2, NBLK, BLK, NRHS)
        assembled = assembled.at[:, boundary_lists[child]].add(blocks)
    root_right = (root_rhs.astype(jnp.float32) - assembled.reshape(2, R, NRHS)).astype(jnp.bfloat16)
    root_real = plain_dot(root_inverse[0], root_right[0]) - plain_dot(root_inverse[1], root_right[1])
    root_imag = plain_dot(root_inverse[0], root_right[1]) + plain_dot(root_inverse[1], root_right[0])
    return jnp.concatenate(solutions, axis=2), jnp.stack((root_real, root_imag))
```

```python
import functools

import jax
import jax.numpy as jnp
from jax import lax
from jax.experimental import pallas as pl
from jax.experimental.pallas import tpu as pltpu
from jax.sharding import PartitionSpec as P

BLK = 128
GROUP = 16
CAP = 13
F32 = jnp.float32
BF16 = jnp.bfloat16
PLAIN = (((1,), (0,)), ((), ()))
TURNED = (((1,), (1,)), ((), ()))
LIMIT = 48 * 2**20
SMEM = pl.BlockSpec(memory_space=pltpu.SMEM)
VMEM = pl.BlockSpec(memory_space=pltpu.VMEM)
HBM = pl.BlockSpec(memory_space=pltpu.HBM)


def call(kernel, name, scalars, arrays, out_shape, weights=(), flops=0, scratch=()):
    moved = sum(a.size * a.dtype.itemsize for a in (*arrays, *weights, *out_shape))
    return pl.pallas_call(
        kernel,
        in_specs=[SMEM] * len(scalars) + [VMEM] * len(arrays) + [HBM] * len(weights),
        out_specs=[VMEM] * len(out_shape),
        out_shape=list(out_shape),
        scratch_shapes=list(scratch),
        compiler_params=pltpu.CompilerParams(vmem_limit_bytes=LIMIT),
        cost_estimate=pl.CostEstimate(flops=flops, bytes_accessed=moved, transcendentals=0),
        name=name,
    )(*scalars, *arrays, *weights)


def shape(dims, dtype=F32):
    return jax.ShapeDtypeStruct(dims, dtype)


def after(x, *earlier):
    return lax.optimization_barrier((x, *earlier))[0]


def flip(x, axis, bit):
    return lax.ppermute(x, axis, [(i, i ^ 1 << bit) for i in range(lax.axis_size(axis))])


def tile_of(size, most):
    return max(t for t in range(BLK, most + 1, BLK) if size % t == 0)


def orders(levels):
    return (tuple(range(levels)), tuple(reversed(range(levels))))


def tables(chip, core, lists, rows, per_row, chips, per_chip):
    per_core = per_chip // 2
    targets = lists.reshape(rows, per_row)
    k = targets // per_chip
    ids = jnp.arange(per_row)
    same = (k[:, :, None] == k[:, None, :]) & (ids[None, :] < ids[:, None])
    rank = jnp.sum(same.astype(jnp.int32), axis=2)
    place = targets % per_chip
    owner = place // per_core
    spot = (owner ^ core) * per_core + place - owner * per_core
    slots = jnp.arange(per_chip)[None, :, None]
    here = (k == chip)[:, None, :] & (rank[:, None, :] == slots)
    dest = per_chip + jnp.sum(jnp.where(here, spot[:, None, :] - per_chip, 0), axis=2)
    return rank.reshape(-1), dest.reshape(-1), jnp.max(rank) + 1


def complex_product(left, by_real, by_imag, dims):
    n = left.shape[0] // 2
    one = lax.dot_general(left, by_real, dims, preferred_element_type=F32)
    two = lax.dot_general(left, by_imag, dims, preferred_element_type=F32)
    return one[:n] - two[n:], one[n:] + two[:n]


def load(copies, ahead):
    state = [0, 0]

    def start(until):
        for copy in copies[state[0] : until]:
            copy.start()
        state[0] = max(state[0], min(until, len(copies)))

    def take(count=1):
        for _ in range(count):
            copies[state[1]].wait()
            state[1] += 1
            start(state[1] + ahead)

    start(ahead)
    return take


def tile_copies(weights_ref, held_ref, sems, tile):
    spans = [pl.ds(first, tile) for first in range(0, weights_ref.shape[1], tile)]
    return [
        pltpu.make_async_copy(weights_ref.at[:, span], held_ref.at[:, span], sems.at[i])
        for i, span in enumerate(spans)
    ]


def child_kernel(places, chips, tile, me_ref, *refs):
    blocks = refs[: len(places)]
    weights_ref, keep_ref, first_ref, second_ref, left_ref, held_ref, sems = refs[len(places) :]
    _, depth, width = weights_ref.shape
    copies = []
    for first in range(0, width, tile):
        for begin in (0, depth // 2):
            at = (slice(None), pl.ds(begin, depth // 2), pl.ds(first, tile))
            copies.append(pltpu.make_async_copy(weights_ref.at[at], held_ref.at[at], sems.at[len(copies)]))
    take = load(copies, 3)
    chip = me_ref[1] // 2
    for (part, side, distances), block in zip(places, blocks):
        for at, distance in enumerate(distances):
            left_ref[(part * 2 + side) * chips + (chip ^ distance)] = block[at]
    left = left_ref[...].reshape(-1, depth)
    n = left.shape[0] // 2
    for first in range(0, width, tile):
        lanes = slice(first, first + tile)
        values = None
        for begin in (0, depth // 2):
            span = slice(begin, begin + depth // 2)
            take()
            more = complex_product(left[:, span], held_ref[0, span, lanes], held_ref[1, span, lanes], PLAIN)
            values = more if values is None else tuple(a + b for a, b in zip(values, more))
        send_ref, lanes_sent = (first_ref, lanes)
        if first >= width // 2:
            send_ref, lanes_sent = (second_ref, slice(first - width // 2, first - width // 2 + tile))
        for part, value in enumerate(values):
            keep_ref[part * n : (part + 1) * n, lanes] = value
            send_ref[part * n : (part + 1) * n, lanes_sent] = value.astype(BF16)


def child_product(me, places, blocks, weights, chips):
    _, depth, width = weights.shape
    group = blocks[0].shape[1]
    n2 = 4 * chips * group
    tile = tile_of(width // 2, 256)
    half = shape((n2, width // 2), BF16)
    return call(
        functools.partial(child_kernel, places, chips, tile),
        "child_product",
        (me,),
        blocks,
        (shape((n2, width)), half, half),
        weights=(weights,),
        flops=4 * n2 * depth * width,
        scratch=(
            pltpu.VMEM((4 * chips, group, depth), BF16),
            pltpu.VMEM(weights.shape, BF16),
            pltpu.SemaphoreType.DMA((2 * (width // tile),)),
        ),
    )


def update_kernel(cap, per_row, per_chip, tile, me_ref, lists_ref, rank_ref, half_ref, *refs):
    got_refs, weights_ref, (y_ref, *parts), held_ref, sems = refs[:2], refs[2], refs[3:8], *refs[8:]
    take = load(tile_copies(weights_ref, held_ref, sems, tile), 3)
    for i, ref in enumerate(got_refs):
        lanes = slice(i * ref.shape[1], (i + 1) * ref.shape[1])
        y_ref[:, lanes] = (half_ref[:, lanes] + ref[...].astype(F32)).astype(BF16)
    y = y_ref[...]
    n = y.shape[0] // 4
    chip = me_ref[1] // 2
    spare = parts[0].shape[0] - 1
    for i in range(weights_ref.shape[1] // tile):
        span = slice(i * tile, (i + 1) * tile)
        take()
        values = complex_product(y, held_ref[0, span], held_ref[1, span], TURNED)
        for t in range(tile // BLK):
            at = me_ref[0] * per_row + i * (tile // BLK) + t
            rank = rank_ref[at]
            slot = jnp.where(rank < cap, (lists_ref[at] // per_chip ^ chip) * cap + rank, spare)
            for value, keep_ref, send_ref in zip(values, parts[:2], parts[2:]):
                block = value[:, t * BLK : (t + 1) * BLK]
                keep_ref[slot] = block[:n]
                send_ref[slot] = block[n:].astype(BF16)


def update_product(me, lists, rank, half, gots, weights, cap, chips, per_row, per_chip):
    _, rows, depth = weights.shape
    tile = tile_of(rows, 512)
    dims = (chips * cap + 1, half.shape[0] // 4, BLK)
    return call(
        functools.partial(update_kernel, cap, per_row, per_chip, tile),
        "update_product",
        (me, lists, rank),
        (half, *gots),
        (shape(half.shape, BF16), shape(dims), shape(dims), shape(dims, BF16), shape(dims, BF16)),
        weights=(weights,),
        flops=4 * half.shape[0] * depth * rows,
        scratch=(pltpu.VMEM(weights.shape, BF16), pltpu.SemaphoreType.DMA((rows // tile,))),
    )


def late_kernel(per_row, per_chip, me_ref, lists_ref, rank_ref, turn_ref, y_ref, weights_ref, *refs):
    parts, (held_ref, sem) = refs[:4], refs[4:]
    n = y_ref.shape[0] // 4
    chip = me_ref[1] // 2
    for ref in parts:
        ref[...] = jnp.zeros_like(ref)

    @pl.loop(0, per_row)
    def _(t):
        at = me_ref[0] * per_row + t

        @pl.when(rank_ref[at] == turn_ref[0])
        def _():
            slot = lists_ref[at] // per_chip ^ chip
            span = pl.ds(pl.multiple_of(t * BLK, BLK), BLK)
            copy = pltpu.make_async_copy(weights_ref.at[:, span], held_ref, sem)
            copy.start()
            copy.wait()
            values = complex_product(y_ref[...], held_ref[0], held_ref[1], TURNED)
            for value, keep_ref, send_ref in zip(values, parts[:2], parts[2:]):
                keep_ref[slot] = value[:n]
                send_ref[slot] = value[n:].astype(BF16)


def late_product(me, lists, rank, turn, y, weights, chips, per_row, per_chip):
    dims = (chips, y.shape[0] // 4, BLK)
    return call(
        functools.partial(late_kernel, per_row, per_chip),
        "late_product",
        (me, lists, rank, turn),
        (y,),
        (shape(dims), shape(dims), shape(dims, BF16), shape(dims, BF16)),
        weights=(weights,),
        flops=4 * y.shape[0] * weights.shape[2] * BLK * chips,
        scratch=(pltpu.VMEM((2, BLK, weights.shape[2]), BF16), pltpu.SemaphoreType.DMA),
    )


def subtract(me_ref, dest_ref, first_rank, pieces, total_ref, per_chip):
    for back, piece in enumerate(pieces):
        first = (me_ref[0] + len(pieces) - back) % len(pieces) * per_chip + first_rank
        for j in range(piece.shape[1]):
            spot = dest_ref[first + j]
            for part in range(2):
                total_ref[spot, part] = total_ref[spot, part] - piece[part, j].astype(F32)


def load_total(base_refs, total_ref):
    per_core = base_refs[0].shape[2] // BLK
    for side, ref in enumerate(base_refs):
        for b in range(per_core):
            total_ref[side * per_core + b] = ref[:, :, b * BLK : (b + 1) * BLK].astype(F32)


def late_subtract_kernel(rows, per_chip, me_ref, dest_ref, turn_ref, own_ref, other_ref, *refs):
    pieces, (own_out, other_out, total_ref) = refs[:rows], refs[rows:]
    load_total((own_ref, other_ref), total_ref)
    subtract(me_ref, dest_ref, turn_ref[0], pieces, total_ref, per_chip)
    per_core = per_chip // 2
    for side, ref in enumerate((own_out, other_out)):
        for b in range(per_core):
            ref[:, :, b * BLK : (b + 1) * BLK] = total_ref[side * per_core + b]


def late_subtract(me, dest, turn, own, other, pieces, per_chip):
    n = own.shape[1]
    return call(
        functools.partial(late_subtract_kernel, len(pieces), per_chip),
        "late_subtract",
        (me, dest, turn),
        (own, other, *pieces),
        (shape(own.shape), shape(other.shape)),
        scratch=(pltpu.VMEM((per_chip + 1, 2, n, BLK), F32),),
    )


def assemble_kernel(rows, per_chip, me_ref, dest_ref, own_ref, other_ref, *refs):
    pieces, (own_out, other_out, total_ref) = refs[:rows], refs[rows:]
    load_total((own_ref, other_ref), total_ref)
    subtract(me_ref, dest_ref, 0, pieces, total_ref, per_chip)
    per_core = per_chip // 2
    for b in range(per_core):
        own_out[b] = total_ref[b].astype(BF16)
        other_out[b] = total_ref[per_core + b].astype(BF16)


def assemble(me, dest, own, other, pieces, per_chip):
    n = own.shape[1]
    dims = (per_chip // 2, 2, n, BLK)
    return call(
        functools.partial(assemble_kernel, len(pieces), per_chip),
        "assemble",
        (me, dest),
        (own, other, *pieces),
        (shape(dims, BF16), shape(dims, BF16)),
        flops=4 * per_chip * n * BLK,
        scratch=(pltpu.VMEM((per_chip + 1, 2, n, BLK), F32),),
    )


def root_kernel(tile, own_ref, other_ref, weights_ref, keep_ref, send_ref, left_ref, held_ref, sems):
    take = load(tile_copies(weights_ref, held_ref, sems, tile), 2)
    half = own_ref.shape[2]
    for b in range(own_ref.shape[0]):
        for part in range(2):
            for side, ref in enumerate((own_ref, other_ref)):
                first = (part * 2 + side) * half
                left_ref[first : first + half, b * BLK : (b + 1) * BLK] = ref[b, part]
    left = left_ref[...]
    for i in range(weights_ref.shape[1] // tile):
        span = slice(i * tile, (i + 1) * tile)
        take()
        for part, value in enumerate(complex_product(left, held_ref[0, span], held_ref[1, span], TURNED)):
            keep_ref[part, :, span] = value[:half]
            send_ref[part, :, span] = value[half:].astype(BF16)


def root_product(own, other, weights):
    _, rows, depth = weights.shape
    n = own.shape[2]
    tile = tile_of(rows, 512)
    return call(
        functools.partial(root_kernel, tile),
        "root_product",
        (),
        (own, other),
        (shape((2, n, rows)), shape((2, n, rows), BF16)),
        weights=(weights,),
        flops=16 * n * depth * rows,
        scratch=(
            pltpu.VMEM((4 * n, depth), BF16),
            pltpu.VMEM(weights.shape, BF16),
            pltpu.SemaphoreType.DMA((rows // tile,)),
        ),
    )


def gather_rhs(rhs, levels, fence=()):
    held = [after(rhs[part][None], *fence) for part in range(2)]
    distances = [(0,), (0,)]
    for at in range(levels):
        bits = [order[at] for order in orders(levels)]
        got = [flip(x, "col", bit + 1) for x, bit in zip(held, bits)]
        other = [tuple(x ^ 1 << bit for x in d) for d, bit in zip(distances, bits)]
        if at < levels - 1:
            held = [jnp.concatenate(pair) for pair in zip(held, got)]
            distances = [d + o for d, o in zip(distances, other)]
    return held, got, distances, other


def both_cores(gathered, fence):
    held, got, distances, other = gathered
    places, blocks = [], []
    for arrays, where, earlier in ((held, distances, ()), (got, other, fence)):
        for part, x in enumerate(arrays):
            for side, block in enumerate((x, flip(after(x, *earlier), "col", 0))):
                places.append((part, side, where[part]))
                blocks.append(block)
    return tuple(places), blocks


def sum_over_plane(keeps, gots, levels, count):
    n = keeps[0].shape[1]
    view = (2,) * levels + (count, n, BLK)
    used = count << levels
    totals = [k[:used].reshape(view) + g[:used].reshape(view).astype(F32) for k, g in zip(keeps, gots)]

    def theirs(total, bit):
        return lax.slice_in_dim(total, 1, 2, axis=levels - 1 - bit).astype(BF16)

    def mine(total, bit):
        return lax.slice_in_dim(total, 0, 1, axis=levels - 1 - bit)

    first = [theirs(total, order[0]) for total, order in zip(totals, orders(levels))]
    got = [flip(x, "col", order[0] + 1) for x, order in zip(first, orders(levels))]

    def rest():
        out = []
        for total, order, now in zip(totals, orders(levels), got):
            for at, bit in enumerate(order):
                now = now if at == 0 else flip(theirs(total, bit), "col", bit + 1)
                total = mine(total, bit) + now.astype(F32)
            out.append(total.reshape((count, n, BLK)).astype(BF16))
        return jnp.stack(out)

    return first, got, rest


def round_ring(x, size):
    held = [x]
    for _ in range(1, size):
        held.append(lax.ppermute(held[-1], "row", [(i, (i + 1) % size) for i in range(size)]))
    return held


def reduce_root(keep, send, levels, chip):
    rows = keep.shape[2]
    total = keep + flip(send, "col", 0).astype(F32)
    out = []
    for part, order in enumerate(orders(levels)):
        now = total[part].reshape((2,) * levels + (-1, rows))
        for bit in order:
            axis = levels - 1 - bit
            at = chip >> bit & 1
            mine = lax.dynamic_slice_in_dim(now, at, 1, axis)
            theirs = lax.dynamic_slice_in_dim(now, 1 - at, 1, axis).astype(BF16)
            now = mine + flip(theirs, "col", bit + 1).astype(F32)
        out.append(now.reshape((-1, rows)))
    return jnp.stack(out)


def local(child_rhs, child_inverse_t, boundary_tiles, boundary_lists, root_rhs, root_inverse):
    rows = lax.axis_size("row")
    cols = lax.axis_size("col")
    in_child = rows // 2
    child_levels = in_child.bit_length() - 1
    chips = cols // 2
    levels = chips.bit_length() - 1
    width = child_rhs.shape[2]
    parts = max(1, width // GROUP)
    group = width // parts
    per_row = boundary_tiles.shape[1] // BLK
    per_chip = 2 * (root_rhs.shape[1] // BLK)
    cap = min(CAP, per_chip, per_row)
    row = lax.axis_index("row")
    col = lax.axis_index("col")
    chip = col // 2
    core = col % 2
    me = jnp.stack((row, col)).astype(jnp.int32)
    lists = boundary_lists.reshape(-1)
    rhs = jnp.transpose(child_rhs, (0, 2, 1))

    gathers = []
    for part in range(parts):
        fence = gathers[-1][1] if gathers else ()
        gathers.append(gather_rhs(rhs[:, part * group : (part + 1) * group], levels, fence))
    halves = []
    for part, gathered in enumerate(gathers):
        later = gathers[part + 1] if part < parts - 1 else ((), ())
        places, blocks = both_cores(gathered, [half[0] for half in halves[-1:]])
        blocks[0] = after(blocks[0], *later[0])
        keep, *sends = child_product(me, places, blocks, child_inverse_t, chips)
        gots = [flip(x, "row", 0) for x in (after(x, *later[1]) for x in sends)]
        for level in range(1, child_levels):
            keep = keep + jnp.concatenate(gots, axis=1).astype(F32)
            gots = [flip(x, "row", level) for x in jnp.split(keep.astype(BF16), 2, axis=1)]
        halves.append((keep, gots))
    rank, dest, most = tables(chip, core, after(lists, halves[-1][0]), rows, per_row, chips, per_chip)

    solved, updates = [], []
    first, first_got = (), ()
    for part, (keep, gots) in enumerate(halves):
        y, *sums = update_product(
            me, lists, rank, after(keep, *first), gots, boundary_tiles, cap, chips, per_row, per_chip
        )
        solved.append(y)
        fence = halves[part + 1][1][:1] if part < parts - 1 else first_got
        others = [flip(after(x, *fence), "col", 0) for x in sums[2:]]
        first, first_got, rest = sum_over_plane(sums[:2], others, levels, cap)
        updates.append(rest())

    rings = []
    for update in updates:
        rings.append(round_ring(after(update, *(ring[-1] for ring in rings[-1:])), rows))
    root = jnp.transpose(after(root_rhs, rings[0][1]), (0, 2, 1)).reshape(2, chips, 2, parts, group, -1)
    own_root = lax.dynamic_index_in_dim(root, core, 2, False)
    other_root = flip(lax.dynamic_index_in_dim(root, 1 - core, 2, False), "col", 0)
    roots = []
    for part in range(parts):
        bases = tuple(x[:, :, part].reshape(2, chips * group, -1).astype(F32) for x in (own_root, other_root))

        def late(i, bases, part=part):
            turn = jnp.reshape(i, (1,)).astype(jnp.int32)
            sums = late_product(me, lists, rank, turn, solved[part], boundary_tiles, chips, per_row, per_chip)
            _, _, rest = sum_over_plane(sums[:2], [flip(x, "col", 0) for x in sums[2:]], levels, 1)
            return late_subtract(me, dest, turn, *bases, round_ring(rest(), rows), per_chip)

        if cap < min(per_chip, per_row):
            bases = lax.fori_loop(cap, most, late, bases)
        mine, theirs = assemble(me, dest, *bases, rings[part], per_chip)
        keep, send = root_product(mine, flip(theirs, "col", 0), root_inverse)
        if part < parts - 1:
            send = after(send, rings[part + 1][1])
        roots.append(reduce_root(keep, send, levels, chip))

    share = chips // in_child
    y = jnp.stack(solved).reshape(parts, 2, 2, chips, group, -1)
    y = lax.dynamic_slice_in_dim(y, row % in_child * share, share, 3)
    y = jnp.where(core == 0, y, y[:, :, ::-1])
    y = jnp.transpose(y, (1, 5, 3, 2, 0, 4))
    y = y.reshape(2, y.shape[1], -1)
    return y, jnp.transpose(jnp.concatenate(roots, axis=1), (0, 2, 1))


def solution(mesh):
    return jax.shard_map(
        local,
        mesh=mesh,
        in_specs=(
            P(None, "row", "col"),
            P(None, "row", "col"),
            P(None, "row", "col"),
            P(),
            P(None, "col", None),
            P(None, "row", "col"),
        ),
        out_specs=(P(None, "col", "row"), P(None, "row", "col")),
        check_vma=False,
    )
```

```python
import functools

import jax
import jax.numpy as jnp
from jax import lax
from jax.experimental import pallas as pl
from jax.experimental.pallas import tpu as pltpu
from jax.sharding import PartitionSpec as P

BLK = 128
GROUP = 16
CAP = 13
F32 = jnp.float32
BF16 = jnp.bfloat16
PLAIN = (((1,), (0,)), ((), ()))
TURNED = (((1,), (1,)), ((), ()))
LIMIT = 22 * 2**20
COST = 8
SMEM = pl.BlockSpec(memory_space=pltpu.SMEM)
VMEM = pl.BlockSpec(memory_space=pltpu.VMEM)
ANY = pl.BlockSpec(memory_space=pl.ANY)


def call(kernel, name, scalars, arrays, out_shape, far=(), deps=(), flops=0, scratch=()):
    moved = sum(a.size * a.dtype.itemsize for a in (*arrays, *far))
    first = len(scalars) + len(arrays) + len(far)
    skip = slice(first, first + len(deps))

    def body(*refs):
        kernel(*refs[: skip.start], *refs[skip.stop :])

    return pl.pallas_call(
        body,
        in_specs=[SMEM] * len(scalars) + [VMEM] * len(arrays) + [ANY] * (len(far) + len(deps)),
        out_specs=[VMEM] * len(out_shape),
        out_shape=list(out_shape),
        scratch_shapes=list(scratch),
        compiler_params=pltpu.CompilerParams(vmem_limit_bytes=LIMIT),
        cost_estimate=pl.CostEstimate(flops=flops // COST, bytes_accessed=moved // COST, transcendentals=0),
        name=name,
    )(*scalars, *arrays, *far, *deps)


def shape(dims, dtype=F32):
    return jax.ShapeDtypeStruct(dims, dtype)


def after(x, *earlier):
    return lax.optimization_barrier((x, *earlier))[0]


def flip(x, axis, bit):
    return lax.ppermute(x, axis, [(i, i ^ 1 << bit) for i in range(lax.axis_size(axis))])


def tile_of(size, most):
    return max(t for t in range(BLK, most + 1, BLK) if size % t == 0)


def orders(levels):
    return (tuple(range(levels)), tuple(reversed(range(levels))))


def tables(chip, core, lists, rows, per_row, chips, per_chip):
    per_core = per_chip // 2
    targets = lists.reshape(rows, per_row)
    k = targets // per_chip
    ids = jnp.arange(per_row)
    same = (k[:, :, None] == k[:, None, :]) & (ids[None, :] < ids[:, None])
    rank = jnp.sum(same.astype(jnp.int32), axis=2)
    place = targets % per_chip
    owner = place // per_core
    spot = (owner ^ core) * per_core + place - owner * per_core
    slots = jnp.arange(per_chip)[None, :, None]
    here = (k == chip)[:, None, :] & (rank[:, None, :] == slots)
    dest = per_chip + jnp.sum(jnp.where(here, spot[:, None, :] - per_chip, 0), axis=2)
    return rank.reshape(-1), dest.reshape(-1), jnp.max(rank) + 1


def complex_product(left, by_real, by_imag, dims):
    n = left.shape[0] // 2
    one = lax.dot_general(left, by_real, dims, preferred_element_type=F32)
    two = lax.dot_general(left, by_imag, dims, preferred_element_type=F32)
    return one[:n] - two[n:], one[n:] + two[:n]


class Weights:
    def __init__(self, parts, ref, held, sems):
        self.size = ref.shape[1] // parts
        self.ref, self.held, self.sems = ref, held, sems
        self.parts = parts
        for i in range(held.shape[0] - 1):
            self.copy(i).start()

    def copy(self, i):
        slot = i % self.held.shape[0]
        return pltpu.make_async_copy(
            self.ref.at[:, pl.ds(i * self.size, self.size)], self.held.at[slot], self.sems.at[slot]
        )

    def wait(self, i):
        self.copy(i).wait()
        following = i + self.held.shape[0] - 1
        if following < self.parts:
            self.copy(following).start()

    def part(self, i, lanes=slice(None)):
        slot = i % self.held.shape[0]
        return self.held[slot, 0, :, lanes], self.held[slot, 1, :, lanes]


def far(weights):
    return (pltpu.with_memory_space_constraint(weights, pltpu.HBM),)


def slots(weights, parts, count):
    count = min(count, parts)
    held = (count, 2, weights.shape[1] // parts, weights.shape[2])
    return (pltpu.VMEM(held, weights.dtype), pltpu.SemaphoreType.DMA((count,)))


def child_kernel(places, chips, parts, me_ref, *refs):
    blocks = refs[: len(places)]
    weights_ref, keep_ref, first_ref, second_ref, left_ref, *scratch = refs[len(places) :]
    weights = Weights(parts, weights_ref, *scratch)
    _, depth, width = weights_ref.shape
    chip = me_ref[1] // 2
    for (part, side, distances), block in zip(places, blocks):
        for at, distance in enumerate(distances):
            left_ref[(part * 2 + side) * chips + (chip ^ distance)] = block[at]
    left = left_ref[...].reshape(-1, depth)
    n = left.shape[0] // 2
    tile = tile_of(width, 512)
    for i in range(parts):
        span = slice(i * weights.size, (i + 1) * weights.size)
        weights.wait(i)
        for first in range(0, width, tile):
            lanes = slice(first, first + tile)
            values = complex_product(left[:, span], *weights.part(i, lanes), PLAIN)
            for part, value in enumerate(values):
                rows = slice(part * n, (part + 1) * n)
                keep_ref[rows, lanes] = value if i == 0 else keep_ref[rows, lanes] + value
    first_ref[...] = keep_ref[:, : width // 2].astype(BF16)
    second_ref[...] = keep_ref[:, width // 2 :].astype(BF16)


def child_product(me, places, blocks, weights, chips, deps):
    _, depth, width = weights.shape
    group = blocks[0].shape[1]
    n2 = 4 * chips * group
    parts = 4
    half = shape((n2, width // 2), BF16)
    return call(
        functools.partial(child_kernel, places, chips, parts),
        "child_product",
        (me,),
        blocks,
        (shape((n2, width)), half, half),
        deps=deps,
        flops=4 * n2 * depth * width,
        far=far(weights),
        scratch=(pltpu.VMEM((4 * chips, group, depth), BF16), *slots(weights, parts, 3)),
    )


def update_kernel(cap, per_row, per_chip, tile, me_ref, lists_ref, rank_ref, half_ref, *refs):
    got_refs, weights_ref, (y_ref, *parts), scratch = refs[:2], refs[2], refs[3:8], refs[8:]
    rows = weights_ref.shape[1]
    weights = Weights(rows // tile, weights_ref, *scratch)
    for i, ref in enumerate(got_refs):
        lanes = slice(i * ref.shape[1], (i + 1) * ref.shape[1])
        y_ref[:, lanes] = (half_ref[:, lanes] + ref[...].astype(F32)).astype(BF16)
    y = y_ref[...]
    n = y.shape[0] // 4
    chip = me_ref[1] // 2
    spare = parts[0].shape[0] - 1
    for i in range(rows // tile):
        weights.wait(i)
        values = complex_product(y, *weights.part(i), TURNED)
        for t in range(tile // BLK):
            at = me_ref[0] * per_row + i * (tile // BLK) + t
            rank = rank_ref[at]
            slot = jnp.where(rank < cap, (lists_ref[at] // per_chip ^ chip) * cap + rank, spare)
            for value, keep_ref, send_ref in zip(values, parts[:2], parts[2:]):
                block = value[:, t * BLK : (t + 1) * BLK]
                keep_ref[slot] = block[:n]
                send_ref[slot] = block[n:].astype(BF16)


def update_product(me, lists, rank, half, gots, weights, cap, chips, per_row, per_chip, deps):
    _, rows, depth = weights.shape
    dims = (chips * cap + 1, half.shape[0] // 4, BLK)
    tile = tile_of(rows, 1024)
    return call(
        functools.partial(update_kernel, cap, per_row, per_chip, tile),
        "update_product",
        (me, lists, rank),
        (half, *gots),
        (shape(half.shape, BF16), shape(dims), shape(dims), shape(dims, BF16), shape(dims, BF16)),
        deps=deps,
        flops=4 * half.shape[0] * depth * rows,
        far=far(weights),
        scratch=slots(weights, rows // tile, 3),
    )


def late_kernel(per_row, per_chip, me_ref, lists_ref, rank_ref, turn_ref, y_ref, weights_ref, *refs):
    parts, (held_ref, sem) = refs[:4], refs[4:]
    n = y_ref.shape[0] // 4
    chip = me_ref[1] // 2
    for ref in parts:
        ref[...] = jnp.zeros_like(ref)

    @pl.loop(0, per_row)
    def _(t):
        at = me_ref[0] * per_row + t

        @pl.when(rank_ref[at] == turn_ref[0])
        def _():
            slot = lists_ref[at] // per_chip ^ chip
            span = pl.ds(pl.multiple_of(t * BLK, BLK), BLK)
            copy = pltpu.make_async_copy(weights_ref.at[:, span], held_ref, sem)
            copy.start()
            copy.wait()
            values = complex_product(y_ref[...], held_ref[0], held_ref[1], TURNED)
            for value, keep_ref, send_ref in zip(values, parts[:2], parts[2:]):
                keep_ref[slot] = value[:n]
                send_ref[slot] = value[n:].astype(BF16)


def late_product(me, lists, rank, turn, y, weights, chips, per_row, per_chip):
    dims = (chips, y.shape[0] // 4, BLK)
    return call(
        functools.partial(late_kernel, per_row, per_chip),
        "late_product",
        (me, lists, rank, turn),
        (y,),
        (shape(dims), shape(dims), shape(dims, BF16), shape(dims, BF16)),
        far=(weights,),
        flops=4 * y.shape[0] * weights.shape[2] * BLK * chips,
        scratch=(pltpu.VMEM((2, BLK, weights.shape[2]), BF16), pltpu.SemaphoreType.DMA),
    )


def subtract(me_ref, dest_ref, first_rank, pieces, total_ref, per_chip):
    for back, piece in enumerate(pieces):
        first = (me_ref[0] + len(pieces) - back) % len(pieces) * per_chip + first_rank
        for j in range(piece.shape[1]):
            spot = dest_ref[first + j]
            for part in range(2):
                total_ref[spot, part] = total_ref[spot, part] - piece[part, j].astype(F32)


def load_total(base_refs, total_ref):
    per_core = base_refs[0].shape[2] // BLK
    for side, ref in enumerate(base_refs):
        for b in range(per_core):
            total_ref[side * per_core + b] = ref[:, :, b * BLK : (b + 1) * BLK].astype(F32)


def late_subtract_kernel(rows, per_chip, me_ref, dest_ref, turn_ref, own_ref, other_ref, *refs):
    pieces, (own_out, other_out, total_ref) = refs[:rows], refs[rows:]
    load_total((own_ref, other_ref), total_ref)
    subtract(me_ref, dest_ref, turn_ref[0], pieces, total_ref, per_chip)
    per_core = per_chip // 2
    for side, ref in enumerate((own_out, other_out)):
        for b in range(per_core):
            ref[:, :, b * BLK : (b + 1) * BLK] = total_ref[side * per_core + b]


def late_subtract(me, dest, turn, own, other, pieces, per_chip):
    n = own.shape[1]
    return call(
        functools.partial(late_subtract_kernel, len(pieces), per_chip),
        "late_subtract",
        (me, dest, turn),
        (own, other, *pieces),
        (shape(own.shape), shape(other.shape)),
        scratch=(pltpu.VMEM((per_chip + 1, 2, n, BLK), F32),),
    )


def assemble_kernel(rows, per_chip, me_ref, dest_ref, own_ref, other_ref, *refs):
    pieces, (own_out, other_out, total_ref) = refs[:rows], refs[rows:]
    load_total((own_ref, other_ref), total_ref)
    subtract(me_ref, dest_ref, 0, pieces, total_ref, per_chip)
    per_core = per_chip // 2
    for b in range(per_core):
        own_out[b] = total_ref[b].astype(BF16)
        other_out[b] = total_ref[per_core + b].astype(BF16)


def assemble(me, dest, own, other, pieces, per_chip, deps):
    n = own.shape[1]
    dims = (per_chip // 2, 2, n, BLK)
    return call(
        functools.partial(assemble_kernel, len(pieces), per_chip),
        "assemble",
        (me, dest),
        (own, other, *pieces),
        (shape(dims, BF16), shape(dims, BF16)),
        deps=deps,
        flops=4 * per_chip * n * BLK,
        scratch=(pltpu.VMEM((per_chip + 1, 2, n, BLK), F32),),
    )


def root_kernel(tile, own_ref, other_ref, weights_ref, keep_ref, send_ref, left_ref, *scratch):
    rows = weights_ref.shape[1]
    weights = Weights(rows // tile, weights_ref, *scratch)
    half = own_ref.shape[2]
    for b in range(own_ref.shape[0]):
        for part in range(2):
            for side, ref in enumerate((own_ref, other_ref)):
                first = (part * 2 + side) * half
                left_ref[first : first + half, b * BLK : (b + 1) * BLK] = ref[b, part]
    left = left_ref[...]
    for i in range(rows // tile):
        span = slice(i * tile, (i + 1) * tile)
        weights.wait(i)
        for part, value in enumerate(complex_product(left, *weights.part(i), TURNED)):
            keep_ref[part, :, span] = value[:half]
            send_ref[part, :, span] = value[half:].astype(BF16)


def root_product(own, other, weights):
    _, rows, depth = weights.shape
    n = own.shape[2]
    tile = tile_of(rows, 512)
    return call(
        functools.partial(root_kernel, tile),
        "root_product",
        (),
        (own, other),
        (shape((2, n, rows)), shape((2, n, rows), BF16)),
        flops=16 * n * depth * rows,
        far=far(weights),
        scratch=(pltpu.VMEM((4 * n, depth), BF16), *slots(weights, rows // tile, 4)),
    )


def gather_rhs(rhs, levels, fence=()):
    held = [after(rhs[part][None], *fence) for part in range(2)]
    distances = [(0,), (0,)]
    for at in range(levels):
        bits = [order[at] for order in orders(levels)]
        got = [flip(x, "col", bit + 1) for x, bit in zip(held, bits)]
        other = [tuple(x ^ 1 << bit for x in d) for d, bit in zip(distances, bits)]
        if at < levels - 1:
            held = [jnp.concatenate(pair) for pair in zip(held, got)]
            distances = [d + o for d, o in zip(distances, other)]
    return held, got, distances, other


def both_cores(gathered, fence):
    held, got, distances, other = gathered
    places, blocks = [], []
    for arrays, where, earlier in ((held, distances, ()), (got, other, fence)):
        for part, x in enumerate(arrays):
            for side, block in enumerate((x, flip(after(x, *earlier), "col", 0))):
                places.append((part, side, where[part]))
                blocks.append(block)
    return tuple(places), blocks


def total(terms):
    return functools.reduce(lambda a, b: a + b, [x.astype(F32) for x in terms])


def sum_over_plane(keeps, sends, levels, count):
    n = keeps[0].shape[1]
    view = (2,) * levels + (count, n, BLK)
    used = count << levels
    bits = list(zip(*orders(levels)))
    terms = [[k[:used].reshape(view), flip(x, "col", 0)[:used].reshape(view)] for k, x in zip(keeps, sends)]

    def cut(x, bit, at):
        return lax.slice_in_dim(x, at, at + 1, axis=levels - 1 - bit)

    for at, pair in enumerate(bits):
        theirs = [total([cut(x, bit, 1) for x in xs]).astype(BF16) for xs, bit in zip(terms, pair)]
        if at == 0:
            yield theirs
        gots = [flip(x, "col", bit + 1) for x, bit in zip(theirs, pair)]
        yield gots
        terms = [[cut(x, bit, 0) for x in xs] + [got] for xs, bit, got in zip(terms, pair, gots)]
    yield [jnp.stack([total(xs).reshape((count, n, BLK)).astype(BF16) for xs in terms])]


class Steps:
    def __init__(self, levels):
        self.levels = levels
        self.now = ()

    def next(self):
        for self.now in self.levels:
            return self.now
        return ()

    def finish(self):
        while self.next():
            pass
        return self.now[0]


def ring_step(held, size, fence=()):
    pairs = [(i, (i + 1) % size) for i in range(size)]
    held.append(lax.ppermute(after(held[-1], *fence), "row", pairs))


def reduce_root(keep, send, levels, chip):
    rows = keep.shape[2]
    got = flip(send, "col", 0)
    terms = [[x[part].reshape((2,) * levels + (-1, rows)) for x in (keep, got)] for part in range(2)]

    def cut(x, bit, at):
        return lax.dynamic_slice_in_dim(x, at, 1, levels - 1 - bit)

    for pair in zip(*orders(levels)):
        mine = [chip >> bit & 1 for bit in pair]
        theirs = [
            total([cut(x, bit, 1 - at) for x in xs]).astype(BF16) for xs, bit, at in zip(terms, pair, mine)
        ]
        gots = [flip(x, "col", bit + 1) for x, bit in zip(theirs, pair)]
        yield gots
        terms = [[cut(x, bit, at) for x in xs] + [got] for xs, bit, at, got in zip(terms, pair, mine, gots)]
    yield [jnp.stack([total(xs).reshape((-1, rows)) for xs in terms])]


def local(child_rhs, child_inverse_t, boundary_tiles, boundary_lists, root_rhs, root_inverse):
    rows = lax.axis_size("row")
    cols = lax.axis_size("col")
    in_child = rows // 2
    child_levels = in_child.bit_length() - 1
    chips = cols // 2
    levels = chips.bit_length() - 1
    width = child_rhs.shape[2]
    parts = max(1, width // GROUP)
    group = width // parts
    per_row = boundary_tiles.shape[1] // BLK
    per_chip = 2 * (root_rhs.shape[1] // BLK)
    cap = min(CAP, per_chip, per_row)
    row = lax.axis_index("row")
    col = lax.axis_index("col")
    chip = col // 2
    core = col % 2
    me = jnp.stack((row, col)).astype(jnp.int32)
    lists = boundary_lists.reshape(-1)
    rhs = jnp.transpose(child_rhs, (0, 2, 1))

    def following(arrays, part):
        return arrays[part + 1] if part < parts - 1 else ((), ())

    gathers = []
    for part in range(parts):
        fence = gathers[-1][0] if gathers else ()
        gathers.append(gather_rhs(rhs[:, part * group : (part + 1) * group], levels, fence))
    held = gathers[0][0]
    root = jnp.transpose(after(root_rhs, *held), (0, 2, 1)).reshape(2, chips, 2, parts, group, -1)
    own = lax.dynamic_index_in_dim(root, core, 2, False)
    other = flip(lax.dynamic_index_in_dim(root, 1 - core, 2, False), "col", 0)
    sides = [
        tuple(x[:, :, part].reshape(2, chips * group, -1).astype(F32) for x in (own, other)) for part in range(parts)
    ]
    rank, dest, most = tables(chip, core, after(lists, *held), rows, per_row, chips, per_chip)
    early = (rank, dest, *(x for pair in sides for x in pair))
    halves = []
    for part, gathered in enumerate(gathers):
        later = following(gathers, part)
        earlier = halves[-1][1][:1] if halves else ()
        places, blocks = both_cores(gathered, earlier)
        keep, *sends = child_product(me, places, blocks, child_inverse_t, chips, (*later[0], *early))
        halves.append((keep, [after(x, *later[1]) for x in sends]))
    solutions = []
    for keep, sends in halves:
        fence = solutions[-1][1] if solutions else ()
        gots = [flip(after(x, *fence), "row", 0) for x in sends]
        for level in range(1, child_levels):
            keep = keep + jnp.concatenate(gots, axis=1).astype(F32)
            gots = [flip(x, "row", level) for x in jnp.split(keep.astype(BF16), 2, axis=1)]
        solutions.append((keep, gots))

    solved, sums = [], []
    first, got = (), ()
    for part, (keep, gots) in enumerate(solutions):
        later = following(solutions, part)[1]
        y, *values = update_product(
            me, lists, rank, keep, gots, boundary_tiles, cap, chips, per_row, per_chip, first
        )
        solved.append(y)
        sends = [after(x, *(later[:1] if later else got)) for x in values[2:]]
        steps = Steps(sum_over_plane(values[:2], sends, levels, cap))
        first = steps.next()
        if part == 0:
            got = steps.next()
        sums.append(steps)

    updates = [sums[0].finish()]
    roots, ring = [], []
    for part in range(parts):
        def late(i, bases, part=part):
            turn = jnp.reshape(i, (1,)).astype(jnp.int32)
            values = late_product(me, lists, rank, turn, solved[part], boundary_tiles, chips, per_row, per_chip)
            held = [Steps(sum_over_plane(values[:2], values[2:], levels, 1)).finish()]
            for _ in range(1, rows):
                ring_step(held, rows)
            return late_subtract(me, dest, turn, *bases, held, per_chip)

        ring = [after(updates[part], *ring[-1:])]
        beside = sums[part + 1] if part < parts - 1 else Steps(())
        fence = ()
        for at in range(1, rows):
            ring_step(ring, rows, fence if at > 2 else ())
            if part > 0 and at == 1:
                keep, send = product
                beside = Steps(reduce_root(keep, after(send, ring[-1]), levels, chip))
            else:
                later = beside.next()
                fence = fence or later
        deps = ()
        if part > 0:
            roots.append(beside.finish())
            deps = roots[-1:]
        if part < parts - 1:
            updates.append(sums[part + 1].finish())
            deps = (*deps, updates[-1])
        bases = sides[part]
        if cap < min(per_chip, per_row):
            bases = lax.fori_loop(cap, most, late, bases)
        mine, theirs = assemble(me, dest, *bases, ring, per_chip, deps)
        product = root_product(mine, flip(theirs, "col", 0), root_inverse)
    roots.append(Steps(reduce_root(*product, levels, chip)).finish())

    share = chips // in_child
    y = jnp.stack(solved).reshape(parts, 2, 2, chips, group, -1)
    y = lax.dynamic_slice_in_dim(y, row % in_child * share, share, 3)
    y = jnp.where(core == 0, y, y[:, :, ::-1])
    y = jnp.transpose(y, (1, 5, 3, 2, 0, 4))
    y = y.reshape(2, y.shape[1], -1)
    return y, jnp.transpose(jnp.concatenate(roots, axis=1), (0, 2, 1))


def solution(mesh):
    return jax.shard_map(
        local,
        mesh=mesh,
        in_specs=(
            P(None, "row", "col"),
            P(None, "row", "col"),
            P(None, "row", "col"),
            P(),
            P(None, "col", None),
            P(None, "row", "col"),
        ),
        out_specs=(P(None, "col", "row"), P(None, "row", "col")),
        check_vma=False,
    )
```

```python
import functools

import jax
import jax.numpy as jnp
from jax import lax
from jax.experimental import pallas as pl
from jax.experimental.pallas import tpu as pltpu
from jax.sharding import PartitionSpec as P

BLK = 128
GROUP = 16
CAP = 13
F32 = jnp.float32
BF16 = jnp.bfloat16
PLAIN = (((1,), (0,)), ((), ()))
TURNED = (((1,), (1,)), ((), ()))
LIMIT = 22 * 2**20
COST = 32
SMEM = pl.BlockSpec(memory_space=pltpu.SMEM)
VMEM = pl.BlockSpec(memory_space=pltpu.VMEM)
ANY = pl.BlockSpec(memory_space=pl.ANY)


def call(kernel, name, scalars, arrays, out_shape, far=(), deps=(), flops=0, scratch=()):
    moved = sum(a.size * a.dtype.itemsize for a in (*arrays, *far))
    first = len(scalars) + len(arrays) + len(far)
    skip = slice(first, first + len(deps))

    def body(*refs):
        kernel(*refs[: skip.start], *refs[skip.stop :])

    return pl.pallas_call(
        body,
        in_specs=[SMEM] * len(scalars) + [VMEM] * len(arrays) + [ANY] * (len(far) + len(deps)),
        out_specs=[VMEM] * len(out_shape),
        out_shape=list(out_shape),
        scratch_shapes=list(scratch),
        compiler_params=pltpu.CompilerParams(vmem_limit_bytes=LIMIT),
        cost_estimate=pl.CostEstimate(flops=flops // COST, bytes_accessed=moved // COST, transcendentals=0),
        name=name,
    )(*scalars, *arrays, *far, *deps)


def shape(dims, dtype=F32):
    return jax.ShapeDtypeStruct(dims, dtype)


def after(x, *earlier):
    return lax.optimization_barrier((x, *earlier))[0]


def flip(x, axis, bit):
    return lax.ppermute(x, axis, [(i, i ^ 1 << bit) for i in range(lax.axis_size(axis))])


def tile_of(size, most):
    return max(t for t in range(BLK, most + 1, BLK) if size % t == 0)


def orders(levels):
    return (tuple(range(levels)), tuple(reversed(range(levels))))


def tables(chip, core, lists, rows, per_row, chips, per_chip):
    per_core = per_chip // 2
    targets = lists.reshape(rows, per_row)
    k = targets // per_chip
    ids = jnp.arange(per_row)
    same = (k[:, :, None] == k[:, None, :]) & (ids[None, :] < ids[:, None])
    rank = jnp.sum(same.astype(jnp.int32), axis=2)
    place = targets % per_chip
    owner = place // per_core
    spot = (owner ^ core) * per_core + place - owner * per_core
    slots = jnp.arange(per_chip)[None, :, None]
    here = (k == chip)[:, None, :] & (rank[:, None, :] == slots)
    dest = per_chip + jnp.sum(jnp.where(here, spot[:, None, :] - per_chip, 0), axis=2)
    return rank.reshape(-1), dest.reshape(-1), jnp.max(rank) + 1


def complex_product(left, by_real, by_imag, dims):
    n = left.shape[0] // 2
    one = lax.dot_general(left, by_real, dims, preferred_element_type=F32)
    two = lax.dot_general(left, by_imag, dims, preferred_element_type=F32)
    return one[:n] - two[n:], one[n:] + two[:n]


class Weights:
    def __init__(self, parts, ref, held, sems):
        self.size = ref.shape[1] // parts
        self.ref, self.held, self.sems = ref, held, sems
        self.parts = parts
        for i in range(held.shape[0] - 1):
            self.copy(i).start()

    def copy(self, i):
        slot = i % self.held.shape[0]
        return pltpu.make_async_copy(
            self.ref.at[:, pl.ds(i * self.size, self.size)], self.held.at[slot], self.sems.at[slot]
        )

    def wait(self, i):
        self.copy(i).wait()
        following = i + self.held.shape[0] - 1
        if following < self.parts:
            self.copy(following).start()

    def part(self, i, lanes=slice(None)):
        slot = i % self.held.shape[0]
        return self.held[slot, 0, :, lanes], self.held[slot, 1, :, lanes]


def far(*arrays):
    return tuple(pltpu.with_memory_space_constraint(x, pltpu.HBM) for x in arrays)


def slots(weights, parts, count):
    count = min(count, parts)
    held = (count, 2, weights.shape[1] // parts, weights.shape[2])
    return (pltpu.VMEM(held, weights.dtype), pltpu.SemaphoreType.DMA((count,)))


def child_kernel(places, chips, parts, me_ref, *refs):
    blocks = refs[: len(places)]
    weights_ref, keep_ref, first_ref, second_ref, left_ref, sems, *scratch = refs[len(places) :]
    _, depth, width = weights_ref.shape
    chip = me_ref[1] // 2
    copies = []
    for (kinds, side, distance), block in zip(places, blocks):
        for at, part in enumerate(kinds):
            slot = (part * 2 + side) * chips + (chip ^ distance)
            copies.append(pltpu.make_async_copy(block.at[at], left_ref.at[slot], sems.at[len(copies)]))
            copies[-1].start()
    weights = Weights(parts, weights_ref, *scratch)
    for copy in copies:
        copy.wait()
    left = left_ref[...].reshape(-1, depth)
    n = left.shape[0] // 2
    tile = tile_of(width, 512)
    for i in range(parts):
        span = slice(i * weights.size, (i + 1) * weights.size)
        weights.wait(i)
        for first in range(0, width, tile):
            lanes = slice(first, first + tile)
            values = complex_product(left[:, span], *weights.part(i, lanes), PLAIN)
            for part, value in enumerate(values):
                rows = slice(part * n, (part + 1) * n)
                keep_ref[rows, lanes] = value if i == 0 else keep_ref[rows, lanes] + value
    first_ref[...] = keep_ref[:, : width // 2].astype(BF16)
    second_ref[...] = keep_ref[:, width // 2 :].astype(BF16)


def child_product(me, places, blocks, weights, chips, deps):
    _, depth, width = weights.shape
    group = blocks[0].shape[1]
    n2 = 4 * chips * group
    parts = 4
    half = shape((n2, width // 2), BF16)
    return call(
        functools.partial(child_kernel, places, chips, parts),
        "child_product",
        (me,),
        (),
        (shape((n2, width)), half, half),
        deps=deps,
        flops=4 * n2 * depth * width,
        far=far(*blocks, weights),
        scratch=(
            pltpu.VMEM((4 * chips, group, depth), BF16),
            pltpu.SemaphoreType.DMA((4 * chips,)),
            *slots(weights, parts, 3),
        ),
    )


def update_kernel(cap, per_row, per_chip, tile, me_ref, lists_ref, rank_ref, half_ref, *refs):
    got_refs, weights_ref, (y_ref, *parts), scratch = refs[:2], refs[2], refs[3:8], refs[8:]
    rows = weights_ref.shape[1]
    weights = Weights(rows // tile, weights_ref, *scratch)
    for i, ref in enumerate(got_refs):
        lanes = slice(i * ref.shape[1], (i + 1) * ref.shape[1])
        y_ref[:, lanes] = (half_ref[:, lanes] + ref[...].astype(F32)).astype(BF16)
    y = y_ref[...]
    n = y.shape[0] // 4
    chip = me_ref[1] // 2
    spare = parts[0].shape[0] - 1
    for i in range(rows // tile):
        weights.wait(i)
        values = complex_product(y, *weights.part(i), TURNED)
        for t in range(tile // BLK):
            at = me_ref[0] * per_row + i * (tile // BLK) + t
            rank = rank_ref[at]
            slot = jnp.where(rank < cap, (lists_ref[at] // per_chip ^ chip) * cap + rank, spare)
            for value, keep_ref, send_ref in zip(values, parts[:2], parts[2:]):
                block = value[:, t * BLK : (t + 1) * BLK]
                keep_ref[slot] = block[:n]
                send_ref[slot] = block[n:].astype(BF16)


def update_product(me, lists, rank, half, gots, weights, cap, chips, per_row, per_chip, deps):
    _, rows, depth = weights.shape
    n2 = half.shape[0]
    dims = (chips * cap + 1, n2 // 4, BLK)
    tile = tile_of(rows, 1024)
    return call(
        functools.partial(update_kernel, cap, per_row, per_chip, tile),
        "update_product",
        (me, lists, rank),
        (half, *gots),
        (shape((n2, depth), BF16), shape(dims), shape(dims), shape(dims, BF16), shape(dims, BF16)),
        deps=deps,
        flops=4 * n2 * depth * rows,
        far=far(weights),
        scratch=slots(weights, rows // tile, 3),
    )


def late_kernel(per_row, per_chip, me_ref, lists_ref, rank_ref, turn_ref, y_ref, weights_ref, *refs):
    parts, (held_ref, sem) = refs[:4], refs[4:]
    n = y_ref.shape[0] // 4
    chip = me_ref[1] // 2
    for ref in parts:
        ref[...] = jnp.zeros_like(ref)

    @pl.loop(0, per_row)
    def _(t):
        at = me_ref[0] * per_row + t

        @pl.when(rank_ref[at] == turn_ref[0])
        def _():
            slot = lists_ref[at] // per_chip ^ chip
            span = pl.ds(pl.multiple_of(t * BLK, BLK), BLK)
            copy = pltpu.make_async_copy(weights_ref.at[:, span], held_ref, sem)
            copy.start()
            copy.wait()
            values = complex_product(y_ref[...], held_ref[0], held_ref[1], TURNED)
            for value, keep_ref, send_ref in zip(values, parts[:2], parts[2:]):
                keep_ref[slot] = value[:n]
                send_ref[slot] = value[n:].astype(BF16)


def late_product(me, lists, rank, turn, y, weights, chips, per_row, per_chip):
    dims = (chips, y.shape[0] // 4, BLK)
    return call(
        functools.partial(late_kernel, per_row, per_chip),
        "late_product",
        (me, lists, rank, turn),
        (y,),
        (shape(dims), shape(dims), shape(dims, BF16), shape(dims, BF16)),
        far=(weights,),
        flops=4 * y.shape[0] * weights.shape[2] * BLK * chips,
        scratch=(pltpu.VMEM((2, BLK, weights.shape[2]), BF16), pltpu.SemaphoreType.DMA),
    )


def subtract(me_ref, dest_ref, first_rank, pieces, total_ref, per_chip):
    for back, piece in enumerate(pieces):
        first = me_ref[2 + back] * per_chip + first_rank
        for j in range(piece.shape[1]):
            spot = dest_ref[first + j]
            for part in range(2):
                total_ref[spot, part] = total_ref[spot, part] - piece[part, j].astype(F32)


def load_total(base_refs, total_ref):
    per_core = base_refs[0].shape[2] // BLK
    for side, ref in enumerate(base_refs):
        for b in range(per_core):
            total_ref[side * per_core + b] = ref[:, :, b * BLK : (b + 1) * BLK].astype(F32)


def late_subtract_kernel(rows, per_chip, me_ref, dest_ref, turn_ref, own_ref, other_ref, *refs):
    pieces, (own_out, other_out, total_ref) = refs[:rows], refs[rows:]
    load_total((own_ref, other_ref), total_ref)
    subtract(me_ref, dest_ref, turn_ref[0], pieces, total_ref, per_chip)
    per_core = per_chip // 2
    for side, ref in enumerate((own_out, other_out)):
        for b in range(per_core):
            ref[:, :, b * BLK : (b + 1) * BLK] = total_ref[side * per_core + b]


def late_subtract(me, dest, turn, own, other, pieces, per_chip):
    n = own.shape[1]
    return call(
        functools.partial(late_subtract_kernel, len(pieces), per_chip),
        "late_subtract",
        (me, dest, turn),
        (own, other, *pieces),
        (shape(own.shape), shape(other.shape)),
        scratch=(pltpu.VMEM((per_chip + 1, 2, n, BLK), F32),),
    )


def assemble_kernel(rows, per_chip, me_ref, dest_ref, own_ref, other_ref, *refs):
    pieces, (own_out, other_out, total_ref) = refs[:rows], refs[rows:]
    load_total((own_ref, other_ref), total_ref)
    subtract(me_ref, dest_ref, 0, pieces, total_ref, per_chip)
    per_core = per_chip // 2
    for b in range(per_core):
        own_out[b] = total_ref[b].astype(BF16)
        other_out[b] = total_ref[per_core + b].astype(BF16)


def assemble(me, dest, own, other, pieces, per_chip, deps):
    n = own.shape[1]
    dims = (per_chip // 2, 2, n, BLK)
    return call(
        functools.partial(assemble_kernel, len(pieces), per_chip),
        "assemble",
        (me, dest),
        (own, other, *pieces),
        (shape(dims, BF16), shape(dims, BF16)),
        deps=deps,
        flops=4 * per_chip * n * BLK,
        scratch=(pltpu.VMEM((per_chip + 1, 2, n, BLK), F32),),
    )


def root_kernel(parts, piece, own_ref, other_ref, weights_ref, keep_ref, send_ref, left_ref, *scratch):
    rows = keep_ref.shape[2]
    weights = Weights(parts, weights_ref.at[:, pl.ds(piece * rows, rows)], *scratch)
    half = own_ref.shape[2]
    for b in range(own_ref.shape[0]):
        for part in range(2):
            for side, ref in enumerate((own_ref, other_ref)):
                first = (part * 2 + side) * half
                left_ref[first : first + half, b * BLK : (b + 1) * BLK] = ref[b, part]
    left = left_ref[...]
    for i in range(parts):
        span = slice(i * weights.size, (i + 1) * weights.size)
        weights.wait(i)
        for part, value in enumerate(complex_product(left, *weights.part(i), TURNED)):
            keep_ref[part, :, span] = value[:half]
            send_ref[part, :, span] = value[half:].astype(BF16)


def root_product(own, other, weights, deps, pieces, piece):
    _, rows, depth = weights.shape
    rows = rows // pieces
    n = own.shape[2]
    tile = tile_of(rows, 512)
    held = (min(4, rows // tile), 2, tile, depth)
    return call(
        functools.partial(root_kernel, rows // tile, piece),
        "root_product",
        (),
        (own, other),
        (shape((2, n, rows)), shape((2, n, rows), BF16)),
        deps=deps,
        flops=16 * n * depth * rows,
        far=far(weights),
        scratch=(
            pltpu.VMEM((4 * n, depth), BF16),
            pltpu.VMEM(held, weights.dtype),
            pltpu.SemaphoreType.DMA((held[0],)),
        ),
    )


def gather_near(own, levels):
    return {1 << bit: flip(own, "col", bit + 1) for bit in range(levels)}


def gather_passed(near, levels):
    passed = {}
    for part, order in enumerate(orders(levels)):
        held = {1 << order[0]: near[1 << order[0]][part : part + 1]}
        for bit in order[1:]:
            more = {d ^ 1 << bit: flip(x, "col", bit + 1) for d, x in held.items()}
            passed.update({(part, d): x for d, x in more.items()})
            held |= more
            held[1 << bit] = near[1 << bit][part : part + 1]
    return passed


def both_cores(own, near, passed):
    items = [((0, 1), d, x) for d, x in ((0, own), *near.items())]
    items += [((part,), d, x) for (part, d), x in passed.items()]
    places, blocks = [], []
    for kinds, distance, x in items:
        for side, block in enumerate((x, flip(x, "col", 0))):
            places.append((kinds, side, distance))
            blocks.append(block)
    return tuple(places), blocks


def total(terms):
    return functools.reduce(lambda a, b: a + b, [x.astype(F32) for x in terms])


def sum_over_plane(keeps, sends, levels, count):
    n = keeps[0].shape[1]
    view = (2,) * levels + (count, n, BLK)
    used = count << levels
    bits = list(zip(*orders(levels)))
    terms = [[k[:used].reshape(view), flip(x, "col", 0)[:used].reshape(view)] for k, x in zip(keeps, sends)]

    def cut(x, bit, at):
        return lax.slice_in_dim(x, at, at + 1, axis=levels - 1 - bit)

    for at, pair in enumerate(bits):
        theirs = [total([cut(x, bit, 1) for x in xs]).astype(BF16) for xs, bit in zip(terms, pair)]
        if at == 0:
            yield theirs
        gots = [flip(x, "col", bit + 1) for x, bit in zip(theirs, pair)]
        yield gots
        terms = [[cut(x, bit, 0) for x in xs] + [got] for xs, bit, got in zip(terms, pair, gots)]
    yield [jnp.stack([total(xs).reshape((count, n, BLK)).astype(BF16) for xs in terms])]


class Steps:
    def __init__(self, levels):
        self.levels = levels
        self.now = ()

    def next(self):
        for self.now in self.levels:
            return self.now
        return ()

    def finish(self):
        while self.next():
            pass
        return self.now[0]


def ring_order(size):
    return [0, *range(1, size, 2), *reversed(range(2, size, 2))]


def ring_step(held, size, fence=()):
    order = ring_order(size)
    pairs = list(zip(order, order[1:] + order[:1]))
    held.append(lax.ppermute(after(held[-1], *fence), "row", pairs))


def reduce_root(keep, send, levels, chip):
    rows = keep.shape[2]
    got = flip(send, "col", 0)
    terms = [[x[part].reshape((2,) * levels + (-1, rows)) for x in (keep, got)] for part in range(2)]

    def cut(x, bit, at):
        return lax.dynamic_slice_in_dim(x, at, 1, levels - 1 - bit)

    for pair in zip(*orders(levels)):
        mine = [chip >> bit & 1 for bit in pair]
        theirs = [
            total([cut(x, bit, 1 - at) for x in xs]).astype(BF16) for xs, bit, at in zip(terms, pair, mine)
        ]
        gots = [flip(x, "col", bit + 1) for x, bit in zip(theirs, pair)]
        yield gots
        terms = [[cut(x, bit, at) for x in xs] + [got] for xs, bit, at, got in zip(terms, pair, mine, gots)]
    yield [jnp.stack([total(xs).reshape((-1, rows)) for xs in terms])]


def local(child_rhs, child_inverse_t, boundary_tiles, boundary_lists, root_rhs, root_inverse):
    rows = lax.axis_size("row")
    cols = lax.axis_size("col")
    in_child = rows // 2
    child_levels = in_child.bit_length() - 1
    chips = cols // 2
    levels = chips.bit_length() - 1
    width = child_rhs.shape[2]
    parts = max(1, width // GROUP)
    group = width // parts
    per_row = boundary_tiles.shape[1] // BLK
    per_chip = 2 * (root_rhs.shape[1] // BLK)
    cap = min(CAP, per_chip, per_row)
    row = lax.axis_index("row")
    col = lax.axis_index("col")
    chip = col // 2
    core = col % 2
    order = ring_order(rows)
    befores = [[order[(order.index(r) - back) % rows] for back in range(rows)] for r in range(rows)]
    before = lax.dynamic_index_in_dim(jnp.array(befores, jnp.int32), row, 0, False)
    me = jnp.concatenate((jnp.stack((row, col)), before)).astype(jnp.int32)
    lists = boundary_lists.reshape(-1)
    rhs = jnp.transpose(child_rhs, (0, 2, 1))

    columns = [rhs[:, part * group : (part + 1) * group] for part in range(parts)]
    near = gather_near(columns[0], levels)
    passed = gather_passed(near, levels)
    root = jnp.transpose(root_rhs, (0, 2, 1)).reshape(2, chips, 2, parts, group, -1)
    own = lax.dynamic_index_in_dim(root, core, 2, False)
    other = flip(lax.dynamic_index_in_dim(root, 1 - core, 2, False), "col", 0)
    sides = [
        tuple(x[:, :, part].reshape(2, chips * group, -1).astype(F32) for x in (own, other)) for part in range(parts)
    ]
    rank, dest, most = tables(chip, core, lists, rows, per_row, chips, per_chip)
    solutions = []
    for part in range(parts):
        places, blocks = both_cores(columns[part], near, passed)
        if part < parts - 1:
            near = gather_near(after(columns[part + 1], *passed.values()), levels)
        fence = solutions[-1][1] if solutions else ()
        early = (rank, dest, *(x for pair in sides for x in pair)) if part == 0 else ()
        keep, *sends = child_product(me, places, blocks, child_inverse_t, chips, early)
        if part < parts - 1:
            near = {at: after(x, sends[0]) for at, x in near.items()}
            passed = gather_passed(near, levels)
        gots = [flip(after(x, *fence), "row", 0) for x in sends]
        for level in range(1, child_levels):
            keep = keep + jnp.concatenate(gots, axis=1).astype(F32)
            gots = [flip(x, "row", level) for x in jnp.split(keep.astype(BF16), 2, axis=1)]
        solutions.append((keep, gots))

    solved, sums = [], []
    first, got = (), ()
    for part, (keep, gots) in enumerate(solutions):
        later = solutions[part + 1][1] if part < parts - 1 else ()
        y, *values = update_product(
            me, lists, rank, keep, gots, boundary_tiles, cap, chips, per_row, per_chip, first
        )
        solved.append(y)
        sends = [after(x, *(later[:1] if later else got)) for x in values[2:]]
        steps = Steps(sum_over_plane(values[:2], sends, levels, cap))
        first = steps.next()
        if part == 0:
            got = steps.next()
        sums.append(steps)

    updates = [sums[0].finish()]
    roots = []

    for part in range(parts):
        def late(i, bases, part=part):
            turn = jnp.reshape(i, (1,)).astype(jnp.int32)
            values = late_product(me, lists, rank, turn, solved[part], boundary_tiles, chips, per_row, per_chip)
            held = [Steps(sum_over_plane(values[:2], values[2:], levels, 1)).finish()]
            for _ in range(1, rows):
                ring_step(held, rows)
            return late_subtract(me, dest, turn, *bases, held, per_chip)

        ring = [updates[part]]
        beside = sums[part + 1] if part < parts - 1 else Steps(())
        fence = ()
        for at in range(1, rows):
            ring_step(ring, rows, fence if at > 2 else ())
            if part > 0 and at == 1:
                keep, send = product
                beside = Steps(reduce_root(keep, after(send, ring[-1]), levels, chip))
            else:
                later = beside.next()
                fence = fence or later
        deps = ()
        if part > 0:
            roots.append(beside.finish())
            deps = roots[-1:]
        if part < parts - 1:
            updates.append(sums[part + 1].finish())
            deps = (*deps, updates[-1])
        bases = sides[part]
        if cap < min(per_chip, per_row):
            bases = lax.fori_loop(cap, most, late, bases)
        mine, theirs = assemble(me, dest, *bases, ring, per_chip, deps)
        theirs = flip(theirs, "col", 0)
        if part < parts - 1:
            product = root_product(mine, theirs, root_inverse, (), 1, 0)
    pieces = []
    for piece in range(2):
        earlier = [x[1] for x in pieces]
        pieces.append(root_product(mine, theirs, root_inverse, earlier, 2, piece))
    steps = [Steps(reduce_root(*product, levels, chip)) for product in pieces]
    roots.append(jnp.concatenate([x.finish() for x in steps], axis=2))

    share = chips // in_child
    y = jnp.stack(solved).reshape(parts, 2, 2, chips, group, -1)
    y = lax.dynamic_slice_in_dim(y, row % in_child * share, share, 3)
    y = jnp.where(core == 0, y, y[:, :, ::-1])
    y = jnp.transpose(y, (1, 5, 3, 2, 0, 4))
    y = y.reshape(2, y.shape[1], -1)
    return y, jnp.transpose(jnp.concatenate(roots, axis=1), (0, 2, 1))


def solution(mesh):
    return jax.shard_map(
        local,
        mesh=mesh,
        in_specs=(
            P(None, "row", "col"),
            P(None, "row", "col"),
            P(None, "row", "col"),
            P(),
            P(None, "col", None),
            P(None, "row", "col"),
        ),
        out_specs=(P(None, "col", "row"), P(None, "row", "col")),
        check_vma=False,
    )
```

```python
import functools

import jax
import jax.numpy as jnp
from jax import lax
from jax.experimental import pallas as pl
from jax.experimental.pallas import tpu as pltpu
from jax.sharding import PartitionSpec as P

BLK = 128
GROUP = 16
CAP = 13
F32 = jnp.float32
BF16 = jnp.bfloat16
PLAIN = (((1,), (0,)), ((), ()))
TURNED = (((1,), (1,)), ((), ()))
LIMIT = 22 * 2**20
COST = 32
SMEM = pl.BlockSpec(memory_space=pltpu.SMEM)
VMEM = pl.BlockSpec(memory_space=pltpu.VMEM)
ANY = pl.BlockSpec(memory_space=pl.ANY)


def call(kernel, name, scalars, arrays, out_shape, far=(), deps=(), flops=0, scratch=()):
    moved = sum(a.size * a.dtype.itemsize for a in (*arrays, *far))
    first = len(scalars) + len(arrays) + len(far)
    skip = slice(first, first + len(deps))

    def body(*refs):
        kernel(*refs[: skip.start], *refs[skip.stop :])

    return pl.pallas_call(
        body,
        in_specs=[SMEM] * len(scalars) + [VMEM] * len(arrays) + [ANY] * (len(far) + len(deps)),
        out_specs=[VMEM] * len(out_shape),
        out_shape=list(out_shape),
        scratch_shapes=list(scratch),
        compiler_params=pltpu.CompilerParams(vmem_limit_bytes=LIMIT),
        cost_estimate=pl.CostEstimate(flops=flops // COST, bytes_accessed=moved // COST, transcendentals=0),
        name=name,
    )(*scalars, *arrays, *far, *deps)


def shape(dims, dtype=F32):
    return jax.ShapeDtypeStruct(dims, dtype)


def after(x, *earlier):
    return lax.optimization_barrier((x, *earlier))[0]


def flip(x, axis, bit):
    return lax.ppermute(x, axis, [(i, i ^ 1 << bit) for i in range(lax.axis_size(axis))])


def tile_of(size, most):
    return max(t for t in range(BLK, most + 1, BLK) if size % t == 0)


def orders(levels):
    return (tuple(range(levels)), tuple(reversed(range(levels))))


def tables(chip, core, lists, rows, per_row, chips, per_chip):
    per_core = per_chip // 2
    targets = lists.reshape(rows, per_row)
    k = targets // per_chip
    ids = jnp.arange(per_row)
    same = (k[:, :, None] == k[:, None, :]) & (ids[None, :] < ids[:, None])
    rank = jnp.sum(same.astype(jnp.int32), axis=2)
    place = targets % per_chip
    owner = place // per_core
    spot = (owner ^ core) * per_core + place - owner * per_core
    slots = jnp.arange(per_chip)[None, :, None]
    here = (k == chip)[:, None, :] & (rank[:, None, :] == slots)
    dest = per_chip + jnp.sum(jnp.where(here, spot[:, None, :] - per_chip, 0), axis=2)
    return rank.reshape(-1), dest.reshape(-1), jnp.max(rank) + 1


def complex_product(left, by_real, by_imag, dims):
    n = left.shape[0] // 2
    one = lax.dot_general(left, by_real, dims, preferred_element_type=F32)
    two = lax.dot_general(left, by_imag, dims, preferred_element_type=F32)
    return one[:n] - two[n:], one[n:] + two[:n]


class Weights:
    def __init__(self, parts, ref, held, sems):
        self.size = ref.shape[1] // parts
        self.ref, self.held, self.sems = ref, held, sems
        self.parts = parts
        for i in range(held.shape[0] - 1):
            self.copy(i).start()

    def copy(self, i):
        slot = i % self.held.shape[0]
        return pltpu.make_async_copy(
            self.ref.at[:, pl.ds(i * self.size, self.size)], self.held.at[slot], self.sems.at[slot]
        )

    def wait(self, i):
        self.copy(i).wait()
        following = i + self.held.shape[0] - 1
        if following < self.parts:
            self.copy(following).start()

    def part(self, i, lanes=slice(None)):
        slot = i % self.held.shape[0]
        return self.held[slot, 0, :, lanes], self.held[slot, 1, :, lanes]


def far(*arrays):
    return tuple(pltpu.with_memory_space_constraint(x, pltpu.HBM) for x in arrays)


def slots(weights, parts, count):
    count = min(count, parts)
    held = (count, 2, weights.shape[1] // parts, weights.shape[2])
    return (pltpu.VMEM(held, weights.dtype), pltpu.SemaphoreType.DMA((count,)))


def child_kernel(places, chips, parts, me_ref, *refs):
    blocks = refs[: len(places)]
    weights_ref, keep_ref, first_ref, second_ref, left_ref, sems, *scratch = refs[len(places) :]
    _, depth, width = weights_ref.shape
    chip = me_ref[1] // 2
    copies = []
    for (kinds, side, distance), block in zip(places, blocks):
        for at, part in enumerate(kinds):
            slot = (part * 2 + side) * chips + (chip ^ distance)
            copies.append(pltpu.make_async_copy(block.at[at], left_ref.at[slot], sems.at[len(copies)]))
            copies[-1].start()
    weights = Weights(parts, weights_ref, *scratch)
    for copy in copies:
        copy.wait()
    left = left_ref[...].reshape(-1, depth)
    n = left.shape[0] // 2
    tile = tile_of(width, 512)
    for i in range(parts):
        span = slice(i * weights.size, (i + 1) * weights.size)
        weights.wait(i)
        for first in range(0, width, tile):
            lanes = slice(first, first + tile)
            values = complex_product(left[:, span], *weights.part(i, lanes), PLAIN)
            for part, value in enumerate(values):
                rows = slice(part * n, (part + 1) * n)
                keep_ref[rows, lanes] = value if i == 0 else keep_ref[rows, lanes] + value
    first_ref[...] = keep_ref[:, : width // 2].astype(BF16)
    second_ref[...] = keep_ref[:, width // 2 :].astype(BF16)


def child_product(me, places, blocks, weights, chips, deps):
    _, depth, width = weights.shape
    group = blocks[0].shape[1]
    n2 = 4 * chips * group
    parts = 4
    half = shape((n2, width // 2), BF16)
    return call(
        functools.partial(child_kernel, places, chips, parts),
        "child_product",
        (me,),
        (),
        (shape((n2, width)), half, half),
        deps=deps,
        flops=4 * n2 * depth * width,
        far=far(*blocks, weights),
        scratch=(
            pltpu.VMEM((4 * chips, group, depth), BF16),
            pltpu.SemaphoreType.DMA((4 * chips,)),
            *slots(weights, parts, 3),
        ),
    )


def update_kernel(cap, per_row, per_chip, tile, me_ref, lists_ref, rank_ref, half_ref, *refs):
    got_refs, weights_ref, (y_ref, *parts), scratch = refs[:2], refs[2], refs[3:8], refs[8:]
    rows = weights_ref.shape[1]
    weights = Weights(rows // tile, weights_ref, *scratch)
    for i, ref in enumerate(got_refs):
        lanes = slice(i * ref.shape[1], (i + 1) * ref.shape[1])
        y_ref[:, lanes] = (half_ref[:, lanes] + ref[...].astype(F32)).astype(BF16)
    y = y_ref[...]
    n = y.shape[0] // 4
    chip = me_ref[1] // 2
    spare = parts[0].shape[0] - 1
    for i in range(rows // tile):
        weights.wait(i)
        values = complex_product(y, *weights.part(i), TURNED)
        for t in range(tile // BLK):
            at = me_ref[0] * per_row + i * (tile // BLK) + t
            rank = rank_ref[at]
            slot = jnp.where(rank < cap, (lists_ref[at] // per_chip ^ chip) * cap + rank, spare)
            for value, keep_ref, send_ref in zip(values, parts[:2], parts[2:]):
                block = value[:, t * BLK : (t + 1) * BLK]
                keep_ref[slot] = block[:n]
                send_ref[slot] = block[n:].astype(BF16)


def update_product(me, lists, rank, half, gots, weights, cap, chips, per_row, per_chip, deps):
    _, rows, depth = weights.shape
    n2 = half.shape[0]
    dims = (chips * cap + 1, n2 // 4, BLK)
    tile = tile_of(rows, 1024)
    return call(
        functools.partial(update_kernel, cap, per_row, per_chip, tile),
        "update_product",
        (me, lists, rank),
        (half, *gots),
        (shape((n2, depth), BF16), shape(dims), shape(dims), shape(dims, BF16), shape(dims, BF16)),
        deps=deps,
        flops=4 * n2 * depth * rows,
        far=far(weights),
        scratch=slots(weights, rows // tile, 3),
    )


def late_kernel(per_row, per_chip, me_ref, lists_ref, rank_ref, turn_ref, y_ref, weights_ref, *refs):
    parts, (held_ref, sem) = refs[:4], refs[4:]
    n = y_ref.shape[0] // 4
    chip = me_ref[1] // 2
    for ref in parts:
        ref[...] = jnp.zeros_like(ref)

    @pl.loop(0, per_row)
    def _(t):
        at = me_ref[0] * per_row + t

        @pl.when(rank_ref[at] == turn_ref[0])
        def _():
            slot = lists_ref[at] // per_chip ^ chip
            span = pl.ds(pl.multiple_of(t * BLK, BLK), BLK)
            copy = pltpu.make_async_copy(weights_ref.at[:, span], held_ref, sem)
            copy.start()
            copy.wait()
            values = complex_product(y_ref[...], held_ref[0], held_ref[1], TURNED)
            for value, keep_ref, send_ref in zip(values, parts[:2], parts[2:]):
                keep_ref[slot] = value[:n]
                send_ref[slot] = value[n:].astype(BF16)


def late_product(me, lists, rank, turn, y, weights, chips, per_row, per_chip):
    dims = (chips, y.shape[0] // 4, BLK)
    return call(
        functools.partial(late_kernel, per_row, per_chip),
        "late_product",
        (me, lists, rank, turn),
        (y,),
        (shape(dims), shape(dims), shape(dims, BF16), shape(dims, BF16)),
        far=(weights,),
        flops=4 * y.shape[0] * weights.shape[2] * BLK * chips,
        scratch=(pltpu.VMEM((2, BLK, weights.shape[2]), BF16), pltpu.SemaphoreType.DMA),
    )


def subtract(me_ref, dest_ref, first_rank, pieces, total_ref, per_chip):
    for back, piece in enumerate(pieces):
        first = me_ref[2 + back] * per_chip + first_rank
        for j in range(piece.shape[1]):
            spot = dest_ref[first + j]
            for part in range(2):
                total_ref[spot, part] = total_ref[spot, part] - piece[part, j].astype(F32)


def load_total(base_refs, total_ref):
    per_core = base_refs[0].shape[2] // BLK
    for side, ref in enumerate(base_refs):
        for b in range(per_core):
            total_ref[side * per_core + b] = ref[:, :, b * BLK : (b + 1) * BLK].astype(F32)


def late_subtract_kernel(rows, per_chip, me_ref, dest_ref, turn_ref, own_ref, other_ref, *refs):
    pieces, (own_out, other_out, total_ref) = refs[:rows], refs[rows:]
    load_total((own_ref, other_ref), total_ref)
    subtract(me_ref, dest_ref, turn_ref[0], pieces, total_ref, per_chip)
    per_core = per_chip // 2
    for side, ref in enumerate((own_out, other_out)):
        for b in range(per_core):
            ref[:, :, b * BLK : (b + 1) * BLK] = total_ref[side * per_core + b]


def late_subtract(me, dest, turn, own, other, pieces, per_chip):
    n = own.shape[1]
    return call(
        functools.partial(late_subtract_kernel, len(pieces), per_chip),
        "late_subtract",
        (me, dest, turn),
        (own, other, *pieces),
        (shape(own.shape), shape(other.shape)),
        scratch=(pltpu.VMEM((per_chip + 1, 2, n, BLK), F32),),
    )


def assemble_kernel(rows, per_chip, me_ref, dest_ref, own_ref, other_ref, *refs):
    pieces, (own_out, other_out, total_ref) = refs[:rows], refs[rows:]
    load_total((own_ref, other_ref), total_ref)
    subtract(me_ref, dest_ref, 0, pieces, total_ref, per_chip)
    per_core = per_chip // 2
    for b in range(per_core):
        own_out[b] = total_ref[b].astype(BF16)
        other_out[b] = total_ref[per_core + b].astype(BF16)


def assemble(me, dest, own, other, pieces, per_chip, deps):
    n = own.shape[1]
    dims = (per_chip // 2, 2, n, BLK)
    return call(
        functools.partial(assemble_kernel, len(pieces), per_chip),
        "assemble",
        (me, dest),
        (own, other, *pieces),
        (shape(dims, BF16), shape(dims, BF16)),
        deps=deps,
        flops=4 * per_chip * n * BLK,
        scratch=(pltpu.VMEM((per_chip + 1, 2, n, BLK), F32),),
    )


def root_kernel(parts, piece, own_ref, other_ref, weights_ref, keep_ref, send_ref, left_ref, *scratch):
    rows = keep_ref.shape[2]
    weights = Weights(parts, weights_ref.at[:, pl.ds(piece * rows, rows)], *scratch)
    half = own_ref.shape[2]
    for b in range(own_ref.shape[0]):
        for part in range(2):
            for side, ref in enumerate((own_ref, other_ref)):
                first = (part * 2 + side) * half
                left_ref[first : first + half, b * BLK : (b + 1) * BLK] = ref[b, part]
    left = left_ref[...]
    for i in range(parts):
        span = slice(i * weights.size, (i + 1) * weights.size)
        weights.wait(i)
        for part, value in enumerate(complex_product(left, *weights.part(i), TURNED)):
            keep_ref[part, :, span] = value[:half]
            send_ref[part, :, span] = value[half:].astype(BF16)


def root_product(own, other, weights, deps, pieces, piece):
    _, rows, depth = weights.shape
    rows = rows // pieces
    n = own.shape[2]
    tile = tile_of(rows, 512)
    held = (min(4, rows // tile), 2, tile, depth)
    return call(
        functools.partial(root_kernel, rows // tile, piece),
        "root_product",
        (),
        (own, other),
        (shape((2, n, rows)), shape((2, n, rows), BF16)),
        deps=deps,
        flops=16 * n * depth * rows,
        far=far(weights),
        scratch=(
            pltpu.VMEM((4 * n, depth), BF16),
            pltpu.VMEM(held, weights.dtype),
            pltpu.SemaphoreType.DMA((held[0],)),
        ),
    )


def gather_near(own, levels):
    return {1 << bit: flip(own, "col", bit + 1) for bit in range(levels)}


def gather_passed(near, levels):
    passed = {}
    for part, order in enumerate(orders(levels)):
        held = {1 << order[0]: near[1 << order[0]][part : part + 1]}
        for bit in order[1:]:
            more = {d ^ 1 << bit: flip(x, "col", bit + 1) for d, x in held.items()}
            passed.update({(part, d): x for d, x in more.items()})
            held |= more
            held[1 << bit] = near[1 << bit][part : part + 1]
    return passed


def both_cores(own, near, passed):
    items = [((0, 1), d, x) for d, x in ((0, own), *near.items())]
    items += [((part,), d, x) for (part, d), x in passed.items()]
    places, blocks = [], []
    for kinds, distance, x in items:
        for side, block in enumerate((x, flip(x, "col", 0))):
            places.append((kinds, side, distance))
            blocks.append(block)
    return tuple(places), blocks


def total(terms):
    return functools.reduce(lambda a, b: a + b, [x.astype(F32) for x in terms])


def sum_over_plane(keeps, sends, levels, count):
    n = keeps[0].shape[1]
    view = (2,) * levels + (count, n, BLK)
    used = count << levels
    bits = list(zip(*orders(levels)))
    terms = [[k[:used].reshape(view), flip(x, "col", 0)[:used].reshape(view)] for k, x in zip(keeps, sends)]

    def cut(x, bit, at):
        return lax.slice_in_dim(x, at, at + 1, axis=levels - 1 - bit)

    for at, pair in enumerate(bits):
        theirs = [total([cut(x, bit, 1) for x in xs]).astype(BF16) for xs, bit in zip(terms, pair)]
        if at == 0:
            yield theirs
        gots = [flip(x, "col", bit + 1) for x, bit in zip(theirs, pair)]
        yield gots
        terms = [[cut(x, bit, 0) for x in xs] + [got] for xs, bit, got in zip(terms, pair, gots)]
    yield [jnp.stack([total(xs).reshape((count, n, BLK)).astype(BF16) for xs in terms])]


class Steps:
    def __init__(self, levels):
        self.levels = levels
        self.now = ()

    def next(self):
        for self.now in self.levels:
            return self.now
        return ()

    def finish(self):
        while self.next():
            pass
        return self.now[0]


def ring_order(size):
    return [0, *range(1, size, 2), *reversed(range(2, size, 2))]


def ring_step(held, size, fence=()):
    order = ring_order(size)
    pairs = list(zip(order, order[1:] + order[:1]))
    held.append(lax.ppermute(after(held[-1], *fence), "row", pairs))


def reduce_root(keep, send, levels, chip):
    rows = keep.shape[2]
    got = flip(send, "col", 0)
    terms = [[x[part].reshape((2,) * levels + (-1, rows)) for x in (keep, got)] for part in range(2)]

    def cut(x, bit, at):
        return lax.dynamic_slice_in_dim(x, at, 1, levels - 1 - bit)

    for pair in zip(*orders(levels)):
        mine = [chip >> bit & 1 for bit in pair]
        theirs = [
            total([cut(x, bit, 1 - at) for x in xs]).astype(BF16) for xs, bit, at in zip(terms, pair, mine)
        ]
        gots = [flip(x, "col", bit + 1) for x, bit in zip(theirs, pair)]
        yield gots
        terms = [[cut(x, bit, at) for x in xs] + [got] for xs, bit, at, got in zip(terms, pair, mine, gots)]
    yield [jnp.stack([total(xs).reshape((-1, rows)) for xs in terms])]


def local(child_rhs, child_inverse_t, boundary_tiles, boundary_lists, root_rhs, root_inverse):
    rows = lax.axis_size("row")
    cols = lax.axis_size("col")
    in_child = rows // 2
    child_levels = in_child.bit_length() - 1
    chips = cols // 2
    levels = chips.bit_length() - 1
    width = child_rhs.shape[2]
    parts = max(1, width // GROUP)
    group = width // parts
    per_row = boundary_tiles.shape[1] // BLK
    per_chip = 2 * (root_rhs.shape[1] // BLK)
    cap = min(CAP, per_chip, per_row)
    row = lax.axis_index("row")
    col = lax.axis_index("col")
    chip = col // 2
    core = col % 2
    order = ring_order(rows)
    befores = [[order[(order.index(r) - back) % rows] for back in range(rows)] for r in range(rows)]
    before = lax.dynamic_index_in_dim(jnp.array(befores, jnp.int32), row, 0, False)
    me = jnp.concatenate((jnp.stack((row, col)), before)).astype(jnp.int32)
    lists = boundary_lists.reshape(-1)
    rhs = jnp.transpose(child_rhs, (0, 2, 1))

    columns = [rhs[:, part * group : (part + 1) * group] for part in range(parts)]
    near = gather_near(columns[0], levels)
    passed = gather_passed(near, levels)
    root = jnp.transpose(root_rhs, (0, 2, 1)).reshape(2, chips, 2, parts, group, -1)
    own = lax.dynamic_index_in_dim(root, core, 2, False)
    other = flip(lax.dynamic_index_in_dim(root, 1 - core, 2, False), "col", 0)
    sides = [
        tuple(x[:, :, part].reshape(2, chips * group, -1).astype(F32) for x in (own, other)) for part in range(parts)
    ]
    rank, dest, most = tables(chip, core, lists, rows, per_row, chips, per_chip)
    solutions = []
    for part in range(parts):
        places, blocks = both_cores(columns[part], near, passed)
        if part < parts - 1:
            near = gather_near(after(columns[part + 1], *passed.values()), levels)
        fence = solutions[-1][1] if solutions else ()
        early = (rank, dest, *(x for pair in sides for x in pair)) if part == 0 else ()
        keep, *sends = child_product(me, places, blocks, child_inverse_t, chips, early)
        if part < parts - 1:
            near = {at: after(x, sends[0]) for at, x in near.items()}
            passed = gather_passed(near, levels)
        gots = [flip(after(x, *fence), "row", 0) for x in sends]
        for level in range(1, child_levels):
            keep = keep + jnp.concatenate(gots, axis=1).astype(F32)
            gots = [flip(x, "row", level) for x in jnp.split(keep.astype(BF16), 2, axis=1)]
        solutions.append((keep, gots))

    solved, sums = [], []
    first, got = (), ()
    for part, (keep, gots) in enumerate(solutions):
        later = solutions[part + 1][1] if part < parts - 1 else ()
        y, *values = update_product(
            me, lists, rank, keep, gots, boundary_tiles, cap, chips, per_row, per_chip, first
        )
        solved.append(y)
        sends = [after(x, *(later[:1] if later else got)) for x in values[2:]]
        steps = Steps(sum_over_plane(values[:2], sends, levels, cap))
        first = steps.next()
        if part == 0:
            got = steps.next()
        sums.append(steps)

    updates = [sums[0].finish()]
    roots = []
    for part in range(parts):

        def late(i, bases, part=part):
            turn = jnp.reshape(i, (1,)).astype(jnp.int32)
            values = late_product(me, lists, rank, turn, solved[part], boundary_tiles, chips, per_row, per_chip)
            held = [Steps(sum_over_plane(values[:2], values[2:], levels, 1)).finish()]
            for _ in range(1, rows):
                ring_step(held, rows)
            return late_subtract(me, dest, turn, *bases, held, per_chip)

        ring = [updates[part]]
        beside = sums[part + 1] if part < parts - 1 else Steps(())
        fence = ()
        for at in range(1, rows):
            ring_step(ring, rows, fence if at > 2 and part == 0 else ())
            if part > 0 and at == 1:
                keep, send = product
                beside = Steps(reduce_root(keep, after(send, ring[-1]), levels, chip))
                product = root_product(mine, theirs, root_inverse, ring[-1:], 2, 1)
                rest = Steps(reduce_root(*product, levels, chip))
            else:
                later = beside.next()
                fence = fence or later
        deps = ()
        if part > 0:
            roots.append(jnp.concatenate((beside.finish(), rest.finish()), axis=2))
        if part < parts - 1:
            updates.append(sums[part + 1].finish())
            deps = (*deps, updates[-1])
        bases = sides[part]
        if cap < min(per_chip, per_row):
            bases = lax.fori_loop(cap, most, late, bases)
        mine, theirs = assemble(me, dest, *bases, ring, per_chip, deps)
        theirs = flip(theirs, "col", 0)
        if part < parts - 1:
            product = root_product(mine, theirs, root_inverse, (), 2, 0)
    pieces = []
    for piece in range(2):
        earlier = [x[1] for x in pieces]
        pieces.append(root_product(mine, theirs, root_inverse, earlier, 2, piece))
    steps = [Steps(reduce_root(*product, levels, chip)) for product in pieces]
    roots.append(jnp.concatenate([x.finish() for x in steps], axis=2))

    share = chips // in_child
    y = jnp.stack(solved).reshape(parts, 2, 2, chips, group, -1)
    y = lax.dynamic_slice_in_dim(y, row % in_child * share, share, 3)
    y = jnp.where(core == 0, y, y[:, :, ::-1])
    y = jnp.transpose(y, (1, 5, 3, 2, 0, 4))
    y = y.reshape(2, y.shape[1], -1)
    return y, jnp.transpose(jnp.concatenate(roots, axis=1), (0, 2, 1))


def solution(mesh):
    return jax.shard_map(
        local,
        mesh=mesh,
        in_specs=(
            P(None, "row", "col"),
            P(None, "row", "col"),
            P(None, "row", "col"),
            P(),
            P(None, "col", None),
            P(None, "row", "col"),
        ),
        out_specs=(P(None, "col", "row"), P(None, "row", "col")),
        check_vma=False,
    )
```
